32 devices in a mesh: gx: 4 (over y, x), gy: 8 (over z, core).
Axes of the slice: x: 2, y: 2, z: 4, core: 2. Of those that a mesh axis runs over, the one named last changes fastest.
Arguments:
- white_noise: float32 [4, 4096, 4096], P('gx', 'gy'), may hold values from -6 to 6
- amplitude: float32 [4096, 4096], P(None, 'gy'), may hold values from 0.24 to 1.26, as said below
- offsets: int32 [2], replicated, may hold values from 0 to 7
Outputs:
- trans_x: float32 [4, 4096, 4096], P('gx', 'gy')
- trans_y: float32 [4, 4096, 4096], P('gx', 'gy')
- upscaled: float32 [512, 512], P('gy', 'gx')
The draws below stay inside these ranges and needn't reach their ends.
Inputs may be any that keep to these rules, and one draw needn't show every extreme that they name: amplitude[ky, kx] equals amplitude[(4096 - ky) mod 4096, kx] and amplitude[ky, (4096 - kx) mod 4096]. offsets[0] shifts the coarse blocks along y, offsets[1] along x.
All inputs are finite; a program needn't handle non-finite values.
Results may differ from the reference program's by a relative error of at most 0.000096.
Values sent between devices are 32-bit elements; how exact they have to be, the bound alone decides.
No kernel may reach another device: no remote copies, remote signals or barrier semaphores. Data moves between devices by JAX's collectives and lax.ppermute only.
A program may use at most 192 MiB of HBM per device.

```python
import math
import jax
import jax.numpy as jnp
from jax import lax

NX = 4096
NY = 4096
NZW = 4


def draw_amplitude(key, part):
    base_key = jax.random.fold_in(key, 11)
    table_shape = (NY // 2 + 1, NX // 2 + 1)
    base_table = jnp.exp(jax.random.uniform(base_key, table_shape, jnp.float32, math.log(0.25), math.log(1.25)))
    row_index = jnp.arange(NY, dtype=jnp.int32)
    column_index = jnp.arange(NX, dtype=jnp.int32)
    fold_y = jnp.minimum(row_index, NY - row_index)
    fold_x = jnp.minimum(column_index, NX - column_index)
    return base_table[fold_y[:, None], fold_x[None, :]].astype(jnp.float32)


def level_of(stream_key, extent, shards, smallest, top_value):
    def one(position, parts):
        draws = jax.random.uniform(jax.random.fold_in(jax.random.fold_in(stream_key, 6), position), (parts,), jnp.float32, smallest / len(shards), top_value / len(shards))
        return jnp.repeat(jnp.exp(draws), extent[position] // parts).reshape((-1,) + (1,) * (len(extent) - position - 1))

    gain = one(*shards[0])
    for cut in shards[1:]:
        gain = gain * one(*cut)
    return gain


def noise(stream_key, shape, deviation, reach, shards=(), kind=jnp.bfloat16):
    result = jax.random.normal(stream_key, shape, jnp.float32) * deviation
    if len(shards) > 0:
        result = level_of(stream_key, shape, shards, -0.22, 0.18) * result
    return jnp.clip(result, min=-reach, max=reach).astype(kind)


def setup_inputs(seed: int = 0) -> dict:
    splits = jax.random.split(jax.random.key(seed), 4)
    return {
        "white_noise": noise(splits[0], (NZW, NY, NX), 1.0, 6.0, ((0, 4), (1, 8)), jnp.float32),
        "amplitude": draw_amplitude(jax.random.fold_in(splits[3], 71), 0),
        "offsets": jax.random.randint(splits[2], (2,), 0, 8).astype(jnp.int32),
    }


def realize(one_layer, amplitude):
    spectrum = jnp.fft.fft2(one_layer)
    return jnp.real(jnp.fft.ifft2(spectrum * amplitude)).astype(jnp.float32)

def harmonic(first_cell, second_cell):
    return 2.0 * first_cell * second_cell / (first_cell + second_cell)

def reference(white_noise, amplitude, offsets):
    log_field = lax.map(lambda one_layer: realize(one_layer, amplitude), white_noise)
    permeability = jnp.exp(log_field)
    trans_x = harmonic(permeability, jnp.roll(permeability, -1, axis=2))
    trans_y = harmonic(permeability, jnp.roll(permeability, -1, axis=1))
    column_sums = jnp.stack([lax.optimization_barrier(jnp.sum(permeability, axis=0)), lax.optimization_barrier(jnp.sum(1.0 / permeability, axis=0))])
    shifted = jnp.roll(column_sums, -offsets[0], axis=1)
    shifted = jnp.roll(shifted, -offsets[1], axis=2)
    block_sums = shifted.reshape(2, NY // 8, 8, NX // 8, 8).sum(axis=(2, 4))
    upscaled = jnp.sqrt(block_sums[0] / block_sums[1])
    return (trans_x, trans_y, upscaled)
```

```python
import functools
import math

import jax
import jax.numpy as jnp
import ml_dtypes
import numpy as np
from jax import lax
from jax.experimental import pallas as pl
from jax.experimental.pallas import tpu as pltpu
from jax.sharding import PartitionSpec as P

LANES = 128
RADIX = 32
GROUPS = RADIX // 2
LENGTH = RADIX * LANES
PAIR = 2 * LANES
BLOCK = 8
VMEM_BYTES = 56 * 1024 * 1024

CLASSES = [(0, RADIX // 2)] + [(k, RADIX - k) for k in range(1, GROUPS)]


def pair_matrices():
    lane = np.arange(LANES)[None, :]
    place = np.arange(LANES)[:, None]
    matrices = np.zeros((GROUPS, PAIR, PAIR), np.float64)
    for group, classes in enumerate(CLASSES):
        for half, class_index in enumerate(classes):
            angle = 2.0 * math.pi * (lane * (class_index + RADIX * place) % LENGTH) / LENGTH
            both = np.cos(angle) + np.sin(angle)
            turned = np.sin(angle) - np.cos(angle)
            rows = slice(half * LANES, (half + 1) * LANES)
            if group == 0:
                matrices[0, rows, rows] = both
            else:
                matrices[group, rows, :LANES] = both
                matrices[group, rows, LANES:] = turned if half == 0 else -turned
    return matrices


def two_parts(matrices):
    high = matrices.astype(ml_dtypes.bfloat16)
    low = (matrices - high.astype(np.float64)).astype(ml_dtypes.bfloat16)
    return np.stack([high, low])


@functools.cache
def tables():
    ahead = pair_matrices()
    scale = np.full((GROUPS, 1, 1), 1.0 / (2 * LANES * RADIX))
    scale[0] = 1.0 / (LANES * RADIX)
    back = ahead * scale
    return two_parts(ahead), two_parts(np.swapaxes(ahead, 1, 2)), two_parts(back)


def spread(values):
    count = len(values)
    if count == 1:
        return [values[0]], [None]
    if count == 2:
        return [values[0] + values[1], values[0] - values[1]], [None, None]
    quarter, half = count // 4, count // 2
    even_re, even_im = spread(values[0::2])
    odd_re, odd_im = spread(values[1::2])
    out_re, out_im = [None] * (half + 1), [None] * (half + 1)
    out_re[0] = even_re[0] + odd_re[0]
    out_re[half] = even_re[0] - odd_re[0]
    out_re[quarter] = even_re[quarter]
    out_im[quarter] = -odd_re[quarter]
    for k in range(1, quarter):
        cosine, sine = math.cos(2 * math.pi * k / count), math.sin(2 * math.pi * k / count)
        turned_re = cosine * odd_re[k] + sine * odd_im[k]
        turned_im = cosine * odd_im[k] - sine * odd_re[k]
        out_re[k] = even_re[k] + turned_re
        out_im[k] = even_im[k] + turned_im
        out_re[half - k] = even_re[k] - turned_re
        out_im[half - k] = turned_im - even_im[k]
    return out_re, out_im


def gather(real, imag):
    half = len(real) - 1
    if half == 0:
        return [real[0]]
    if half == 1:
        return [real[0] + real[1], real[0] - real[1]]
    count, quarter = 2 * half, half // 2
    even_re, even_im = [None] * (quarter + 1), [None] * (quarter + 1)
    odd_re, odd_im = [None] * (quarter + 1), [None] * (quarter + 1)
    even_re[0] = real[0] + real[half]
    odd_re[0] = real[0] - real[half]
    even_re[quarter] = real[quarter] + real[quarter]
    odd_re[quarter] = -(imag[quarter] + imag[quarter])
    for k in range(1, quarter):
        cosine, sine = math.cos(2 * math.pi * k / count), math.sin(2 * math.pi * k / count)
        even_re[k] = real[k] + real[half - k]
        even_im[k] = imag[k] - imag[half - k]
        diff_re = real[k] - real[half - k]
        diff_im = imag[k] + imag[half - k]
        odd_re[k] = cosine * diff_re - sine * diff_im
        odd_im[k] = sine * diff_re + cosine * diff_im
    values = [None] * count
    values[0::2] = gather(even_re, even_im)
    values[1::2] = gather(odd_re, odd_im)
    return values


def store_groups(ref, at, values):
    real, imag = spread(values)
    for group in range(GROUPS):
        ref[group, at, :LANES] = real[group]
        ref[group, at, LANES:] = imag[group] if group else real[GROUPS]


def load_groups(ref, at):
    pairs = [(ref[group, at, :LANES], ref[group, at, LANES:]) for group in range(GROUPS)]
    real = [pair[0] for pair in pairs] + [pairs[0][1]]
    imag = [None] + [pair[1] for pair in pairs[1:]] + [None]
    return gather(real, imag)


def halves(value):
    high = value.astype(jnp.bfloat16)
    return high, (value - high.astype(jnp.float32)).astype(jnp.bfloat16)


def dot(left, right, right_axis=0):
    return lax.dot_general(
        left, right, (((1,), (right_axis,)), ((), ())), preferred_element_type=jnp.float32
    )


def times_table(value, table_ref, group):
    high, low = halves(value)
    return dot(high, table_ref[0, group]) + (
        dot(low, table_ref[0, group]) + dot(high, table_ref[1, group])
    )


def strip_at(index):
    return pl.ds(pl.multiple_of(index * BLOCK, BLOCK), BLOCK)


def lanes_of(index):
    return slice(index * LANES, (index + 1) * LANES)


def taken(refs, kinds, count):
    chunks = []
    for stacked in kinds:
        held = 1 if stacked else count
        chunks.append(list(refs[:held]))
        refs = refs[held:]
    return chunks, refs


def view(chunk, stacked, me, step):
    if stacked:
        return step, chunk[0].at[step]
    return me ^ step, chunk[step]


def forward_x(count, cuts, kinds, me_ref, noise_ref, table_ref, *refs):
    outs, (group_ref, spectrum_ref) = taken(refs, kinds, count)
    rows = noise_ref.shape[1]
    share = LANES // count
    me = me_ref[0]

    def strip(index, carry):
        at = strip_at(index)
        store_groups(group_ref, at, [noise_ref[0, at, lanes_of(a)] for a in range(RADIX)])
        return carry

    lax.fori_loop(0, rows // BLOCK, strip, 0, unroll=2)
    for cut, (first, last) in enumerate(cuts):

        def group_step(group, carry, cut=cut, first=first):
            high, low = halves(group_ref[group])
            both = dot(table_ref[0, group], jnp.concatenate([high, low], axis=0), 1)
            spectrum_ref[...] = (both[:, :rows] + both[:, rows:]) + dot(table_ref[1, group], high, 1)
            for step in range(count):
                place, out = view(outs[cut], kinds[cut], me, step)
                for half in range(2):
                    source = pl.multiple_of(half * LANES + place * share, share)
                    target = pl.multiple_of(((group - first) * 2 + half) * share, share)
                    out[pl.ds(target, share), :] = spectrum_ref[pl.ds(source, share), :]
            return carry

        lax.fori_loop(first, last, group_step, 0, unroll=4)


def filter_y(count, in_cuts, in_kinds, out_cuts, out_kinds, gains, me_ref, *refs):
    ins, refs = taken(refs, in_kinds, count)
    gain_refs, (ahead_ref, back_ref) = refs[:gains], refs[gains : gains + 2]
    outs, (field_ref, group_ref) = taken(refs[gains + 2 :], out_kinds, count)
    rows = field_ref.shape[1]
    per = field_ref.shape[2] // LANES
    me = me_ref[0]
    for chunk, stacked, (first, last) in zip(ins, in_kinds, in_cuts):
        for step in range(count):
            place, piece = view(chunk, stacked, me, step)
            field_ref[place, :, first:last] = piece[...]

    def ahead_strip(index, carry):
        at = strip_at(index)
        values = [field_ref[a // per, at, lanes_of(a % per)] for a in range(RADIX)]
        store_groups(group_ref, at, values)
        return carry

    lax.fori_loop(0, rows // BLOCK, ahead_strip, 0, unroll=2)

    def group_step(group, carry):
        spectrum = times_table(group_ref[group], ahead_ref, group)
        other = jnp.where(group == 0, RADIX // 2, RADIX - group)
        columns = [
            pl.ds(pl.multiple_of(place * LANES, LANES), LANES) for place in (group, other)
        ]
        gain = jnp.concatenate(
            [
                jnp.concatenate([ref[0, :, column] for ref in gain_refs], axis=0)
                for column in columns
            ],
            axis=1,
        )
        group_ref[group] = times_table(spectrum * gain, back_ref, group)
        return carry

    lax.fori_loop(0, GROUPS, group_step, 0, unroll=4)

    def back_strip(index, carry):
        at = strip_at(index)
        for a, value in enumerate(load_groups(group_ref, at)):
            field_ref[a // per, at, lanes_of(a % per)] = value
        return carry

    lax.fori_loop(0, rows // BLOCK, back_strip, 0, unroll=2)
    for chunk, stacked, (first, last) in zip(outs, out_kinds, out_cuts):
        for step in range(count):
            place, piece = view(chunk, stacked, me, step)
            piece[...] = field_ref[place, :, first:last]


def inverse_x(
    count, cuts, kinds, layer, start, has_before, has_after, aliased, me_ref, offsets_ref, *refs
):
    ins, refs = taken(refs, kinds, count)
    table_ref, refs = refs[0], refs[1:]
    before_ref = after_ref = None
    if has_before:
        before_ref, refs = refs[0], refs[1:]
    if has_after:
        after_ref, refs = refs[0], refs[1:]
    if aliased:
        refs = refs[2:]
    face_x_hbm, face_y_hbm, sums_ref, first_ref, last_ref, *scratch = refs
    piece_ref, group_ref, upper_ref, lower_ref, face_x, face_y, column_ref, sems = scratch
    rows = face_x.shape[0]
    tiles = rows // BLOCK
    share = LANES // count
    me = me_ref[0]
    lead = 1 if has_before else 0
    made = tiles - 1 + lead + (1 if has_after else 0)
    width = RADIX * LANES

    for chunk, stacked, (first, last) in zip(ins, kinds, cuts):
        span = slice(2 * share * first, 2 * share * last)
        for step in range(count):
            place, piece = view(chunk, stacked, me, step)
            piece_ref[place, span, :] = piece[...]

    def group_step(group, carry):
        parts = []
        for half in range(2):
            at = pl.ds(pl.multiple_of((2 * group + half) * share, share), share)
            parts.append(piece_ref[:, at, :].reshape(LANES, rows))
        stacked = jnp.concatenate(parts, axis=0)
        group_ref[group] = times_table(stacked.T, table_ref, group)
        return carry

    lax.fori_loop(0, GROUPS, group_step, 0, unroll=4)

    def raised(field, at, a):
        upper_ref[at, lanes_of(a)] = jnp.exp(field)
        lower_ref[at, lanes_of(a)] = jnp.exp(-field)

    def field_strip(index, carry, copy_ref=None):
        at = strip_at(index)
        to = strip_at(index + lead)
        for a, value in enumerate(load_groups(group_ref, at)):
            raised(value, to, a)
            if copy_ref is not None:
                copy_ref[:, lanes_of(a)] = value
        return carry

    field_strip(0, 0, first_ref)
    lax.fori_loop(1, tiles - 1, field_strip, 0, unroll=2)
    field_strip(tiles - 1, 0, last_ref)
    for a in range(RADIX):
        if has_before:
            raised(before_ref[:, lanes_of(a)], slice(0, BLOCK), a)
        if has_after:
            end = (lead + tiles) * BLOCK
            raised(after_ref[:, lanes_of(a)], slice(end, end + BLOCK), a)

    row_index = lax.broadcasted_iota(jnp.int32, (BLOCK, LANES), 0)
    lane_index = lax.broadcasted_iota(jnp.int32, (BLOCK, LANES), 1)
    own_rows = row_index >= offsets_ref[0]
    last_row = row_index == BLOCK - 1
    last_lane = lane_index == LANES - 1

    def x_strip(index, carry):
        at = strip_at(index)
        here = [lower_ref[strip_at(index + lead), lanes_of(a)] for a in range(RADIX)]
        moved = [pltpu.roll(value, LANES - 1, 1) for value in here]
        for a in range(RADIX):
            beside = jnp.where(last_lane, moved[(a + 1) % RADIX], moved[a])
            face_x[at, lanes_of(a)] = 2.0 / (here[a] + beside)
        return carry

    lax.fori_loop(0, tiles, x_strip, 0, unroll=2)
    copy_x = pltpu.make_async_copy(
        face_x, face_x_hbm.at[layer, pl.ds(start, rows), :], sems.at[0]
    )
    copy_x.start()

    def add_row(kind, index, a, value):
        at = strip_at(index // BLOCK)
        total = jnp.sum(value, axis=0, keepdims=True)
        column_ref[kind, at, lanes_of(a)] = jnp.where(
            row_index == index % BLOCK, total, column_ref[kind, at, lanes_of(a)]
        )

    def y_strip(index, carry):
        at = strip_at(index)
        then = strip_at(index + 1)
        for a in range(RADIX):
            here, below = lower_ref[at, lanes_of(a)], lower_ref[then, lanes_of(a)]
            moved = pltpu.roll(jnp.where(row_index == 0, below, here), BLOCK - 1, 0)
            face_y[at, lanes_of(a)] = 2.0 / (here + moved)
            add_row(1, index, a, jnp.where(own_rows, here, below))
            here, below = upper_ref[at, lanes_of(a)], upper_ref[then, lanes_of(a)]
            add_row(0, index, a, jnp.where(own_rows, here, below))
        return carry

    lax.fori_loop(0, made, y_strip, 0, unroll=2)
    copy_y = pltpu.make_async_copy(
        face_y, face_y_hbm.at[layer, pl.ds(start - BLOCK * lead, made * BLOCK), :], sems.at[1]
    )
    copy_y.start()

    column_ref[:, :, width:] = column_ref[:, :, :LANES]
    reach = BLOCK * LANES + LANES
    lane = lax.broadcasted_iota(jnp.int32, (reach, LANES), 0)
    block = lax.broadcasted_iota(jnp.int32, (reach, LANES), 1)
    inside = lane - offsets_ref[1] - BLOCK * block
    chosen = jnp.where((inside >= 0) & (inside < BLOCK), 1.0, 0.0).astype(jnp.bfloat16)
    for kind in range(2):
        for part in range(width // (BLOCK * LANES)):
            at = BLOCK * LANES * part
            high, low = halves(column_ref[kind, :, at : at + reach])
            sums_ref[kind, :, lanes_of(part)] = dot(high, chosen) + dot(low, chosen)
    copy_x.wait()
    copy_y.wait()


def exchange(chunk, axis):
    if not isinstance(chunk, list):
        return lax.all_to_all(chunk, axis, 0, 0, tiled=True)
    count = len(chunk)
    arrived = [chunk[0]] + [None] * (count - 1)
    for step in reversed(range(1, count)):
        pairs = [(device, device ^ step) for device in range(count)]
        arrived[step] = lax.ppermute(chunk[step], axis, pairs)
    return arrived


def flat(chunks):
    return [ref for chunk in chunks for ref in (chunk if isinstance(chunk, list) else [chunk])]


def chunked(refs, kinds, count):
    chunks, _ = taken(refs, kinds, count)
    return [chunk[0] if stacked else chunk for chunk, stacked in zip(chunks, kinds)]


def kinds_of(chunks):
    return [not isinstance(chunk, list) for chunk in chunks]


def block_specs(kinds, count, shapes, place_of):
    specs = []
    for number, (stacked, shape) in enumerate(zip(kinds, shapes)):
        place = place_of(number)
        if stacked:
            specs.append(pl.BlockSpec((count, *shape), lambda i, place=place: (0, *place(i))))
        else:
            specs += [pl.BlockSpec(shape, place)] * count
    return specs


def whole_shapes(kinds, count, shapes):
    made = []
    for stacked, shape in zip(kinds, shapes):
        if stacked:
            made.append(jax.ShapeDtypeStruct((count, *shape), jnp.float32))
        else:
            made += [jax.ShapeDtypeStruct(shape, jnp.float32)] * count
    return made


def scalars():
    return pl.BlockSpec(memory_space=pltpu.SMEM)


def params():
    return pltpu.CompilerParams(vmem_limit_bytes=VMEM_BYTES)


def cost(rows, micros):
    return pl.CostEstimate(
        flops=int(rows * micros * 1.15e9 / 256),
        bytes_accessed=rows * LENGTH * 8,
        transcendentals=0,
    )


def run_forward(me, noise, layer, span, cuts, kinds, count, table):
    share = LANES // count
    first, last = span
    step_rows = LANES
    depths = [2 * share * (end - begin) for begin, end in cuts]
    offset = first // step_rows
    outs = pl.pallas_call(
        functools.partial(forward_x, count, cuts, kinds),
        grid=((last - first) // step_rows,),
        in_specs=[
            scalars(),
            pl.BlockSpec((1, step_rows, LENGTH), lambda i: (layer, i + offset, 0)),
            pl.BlockSpec(table.shape, lambda i: (0, 0, 0, 0), pipeline_mode=pl.Buffered(1)),
        ],
        out_specs=block_specs(
            kinds, count, [(depth, step_rows) for depth in depths], lambda n: lambda i: (0, i)
        ),
        out_shape=whole_shapes(kinds, count, [(depth, last - first) for depth in depths]),
        scratch_shapes=[
            pltpu.VMEM((GROUPS, step_rows, PAIR), jnp.float32),
            pltpu.VMEM((PAIR, step_rows), jnp.float32),
        ],
        compiler_params=params(),
        cost_estimate=cost(last - first, 9),
        name="forward_x",
    )(me, noise, table)
    return chunked(outs, kinds, count)


def run_filter(me, chunks, in_cuts, out_cuts, out_kinds, count, gain, span, ahead, back):
    first_row, rows = span.start, span.stop - span.start
    step_rows = min(rows, LANES)
    lane_count = LENGTH // count
    share = LANES // count
    offset = first_row // step_rows
    in_kinds = kinds_of(chunks)
    skips = [offset if flat([chunk])[0].shape[-2] > rows else 0 for chunk in chunks]
    table_spec = pl.BlockSpec(ahead.shape, lambda i: (0, 0, 0, 0), pipeline_mode=pl.Buffered(1))
    gains = step_rows // share

    def gain_place(number):
        def place(i):
            group = (i + offset) * (gains // 2) + number // 2
            if number % 2 == 0:
                return (group, 0, 0)
            return (jnp.where(group == 0, RADIX // 2, RADIX - group), 0, 0)

        return place

    outs = pl.pallas_call(
        functools.partial(filter_y, count, in_cuts, in_kinds, out_cuts, out_kinds, gains),
        grid=(rows // step_rows,),
        in_specs=[scalars()]
        + block_specs(
            in_kinds,
            count,
            [(step_rows, cut[1] - cut[0]) for cut in in_cuts],
            lambda n: lambda i: (i + skips[n], 0),
        )
        + [pl.BlockSpec((1, share, LENGTH), gain_place(n)) for n in range(gains)]
        + [table_spec, table_spec],
        out_specs=block_specs(
            out_kinds,
            count,
            [(step_rows, cut[1] - cut[0]) for cut in out_cuts],
            lambda n: lambda i: (i, 0),
        ),
        out_shape=whole_shapes(out_kinds, count, [(rows, cut[1] - cut[0]) for cut in out_cuts]),
        scratch_shapes=[
            pltpu.VMEM((count, step_rows, lane_count), jnp.float32),
            pltpu.VMEM((GROUPS, step_rows, PAIR), jnp.float32),
        ],
        compiler_params=params(),
        cost_estimate=cost(rows, 16),
        name="filter_y",
    )(me, *flat(chunks), *[gain] * gains, ahead, back)
    return chunked(outs, out_kinds, count)


def run_inverse(
    me, offsets, chunks, lane_starts, cuts, count, layer, span, table, before, after, faces, shape
):
    first, last = span
    rows = last - first
    tiles = rows // BLOCK
    made = tiles - 1 + (before is not None) + (after is not None)
    padded = -(-made // 16) * 16
    held = tiles + (before is not None) + (after is not None)
    kinds = kinds_of(chunks)
    extra = [value for value in (before, after) if value is not None]
    in_specs = [scalars(), scalars()]
    in_specs += block_specs(
        kinds,
        count,
        [(flat([chunk])[0].shape[-2], rows) for chunk in chunks],
        lambda n: lambda i: (0, lane_starts[n] // rows),
    )
    in_specs += [
        pl.BlockSpec(table.shape, lambda i: (0, 0, 0, 0)),
        *[pl.BlockSpec(value.shape, lambda i: (0, 0)) for value in extra],
    ]
    aliases = {}
    if faces is not None:
        aliases = {len(in_specs): 0, len(in_specs) + 1: 1}
        in_specs += [pl.BlockSpec(memory_space=pl.ANY)] * 2
    face = jax.ShapeDtypeStruct(shape, jnp.float32)
    tile = jax.ShapeDtypeStruct((BLOCK, LENGTH), jnp.float32)
    sums_shape = (2, padded, LENGTH // BLOCK)
    face_x, face_y, sums, first_tile, last_tile = pl.pallas_call(
        functools.partial(
            inverse_x,
            count,
            cuts,
            kinds,
            layer,
            first,
            before is not None,
            after is not None,
            faces is not None,
        ),
        grid=(1,),
        in_specs=in_specs,
        out_specs=[
            pl.BlockSpec(memory_space=pl.ANY),
            pl.BlockSpec(memory_space=pl.ANY),
            pl.BlockSpec(sums_shape, lambda i: (0, 0, 0)),
            pl.BlockSpec(tile.shape, lambda i: (0, 0)),
            pl.BlockSpec(tile.shape, lambda i: (0, 0)),
        ],
        out_shape=[face, face, jax.ShapeDtypeStruct(sums_shape, jnp.float32), tile, tile],
        scratch_shapes=[
            pltpu.VMEM((count, LENGTH // count, rows), jnp.float32),
            pltpu.VMEM((GROUPS, rows, PAIR), jnp.float32),
            pltpu.VMEM((held * BLOCK, LENGTH), jnp.float32),
            pltpu.VMEM((held * BLOCK, LENGTH), jnp.float32),
            pltpu.VMEM((rows, LENGTH), jnp.float32),
            pltpu.VMEM((made * BLOCK, LENGTH), jnp.float32),
            pltpu.VMEM((2, padded, LENGTH + LANES), jnp.float32),
            pltpu.SemaphoreType.DMA((2,)),
        ],
        input_output_aliases=aliases,
        compiler_params=params(),
        cost_estimate=cost(rows, 18),
        name="inverse_x",
    )(me, offsets, *flat(chunks), table, *extra, *(faces or ()))
    return (face_x, face_y), sums[:, :made], first_tile, last_tile


def arranged(amplitude, count):
    share = LANES // count
    table = amplitude.reshape(LANES, RADIX, RADIX * share).transpose(1, 0, 2)
    table = lax.optimization_barrier(table).reshape(LENGTH, RADIX * share).T
    return lax.optimization_barrier(table).reshape(share, RADIX, LENGTH).transpose(1, 0, 2)


def sum_scattered(values, axis):
    count = lax.axis_size(axis)
    me = lax.axis_index(axis)
    width = values.shape[-1] // count
    total = lax.dynamic_slice_in_dim(values, me * width, width, values.ndim - 1)
    for step in range(1, count):
        part = lax.dynamic_slice_in_dim(values, (me ^ step) * width, width, values.ndim - 1)
        total = total + lax.ppermute(part, axis, [(d, d ^ step) for d in range(count)])
    return total


def shards(white_noise, amplitude, offsets):
    layers, rows, _ = white_noise.shape
    count = lax.axis_size("gy")
    share = LANES // count
    me = lax.axis_index("gy").reshape(1)
    analysis, ahead, back = [jnp.asarray(table) for table in tables()]
    arrive_spans = [(0, LANES), (LANES, rows)]
    leave_spans = [(0, rows - LANES), (rows - LANES, rows)]
    done_spans = [(at, min(at + 2 * LANES, rows - LANES)) for at in range(0, rows - LANES, 2 * LANES)]
    done_spans.append((rows - LANES, rows))
    cuts = [(0, GROUPS // 2), (GROUPS // 2, GROUPS)]
    every = [(0, GROUPS)]
    gain = None
    faces = None
    totals = None
    for layer in range(layers):
        (early,) = run_forward(me, white_noise, layer, arrive_spans[0], every, [False], count, analysis)
        early = exchange(early, "gy")
        sent = run_forward(me, white_noise, layer, arrive_spans[1], cuts, [False, False], count, analysis)
        if gain is None:
            amplitude, sent = lax.optimization_barrier((amplitude, sent))
            gain = arranged(amplitude, count)
        late = [exchange(part, "gy") for part in sent]
        returned = []
        for cut, (first, last) in enumerate(cuts):
            span = slice(2 * share * first, 2 * share * last)
            out_cuts, out_kinds = ([(0, rows)], [False]) if cut == 0 else (leave_spans, [False, False])
            made = run_filter(
                me,
                [early, late[cut]],
                arrive_spans,
                out_cuts,
                out_kinds,
                count,
                gain,
                span,
                ahead,
                back,
            )
            returned.append([exchange(part, "gy") for part in made])
        before = after = None
        sums = []
        for index, span in enumerate(done_spans):
            final = index == len(done_spans) - 1
            chunks = [returned[0][0], returned[1][1 if final else 0]]
            lane_starts = [span[0], 0 if final else span[0]]
            if final:
                pairs = [(device, (device - 1) % count) for device in range(count)]
                after = lax.ppermute(first_tile, "gy", pairs)
            faces, part, head, before_next = run_inverse(
                me,
                offsets,
                chunks,
                lane_starts,
                cuts,
                count,
                layer,
                span,
                back,
                before,
                after,
                faces,
                white_noise.shape,
            )
            sums.append(part)
            before = before_next
            if index == 0:
                first_tile = head
        blocks = jnp.concatenate(sums, axis=1)
        totals = blocks if totals is None else totals + blocks
    totals = sum_scattered(totals, "gx")
    return faces[0], faces[1], jnp.sqrt(totals[0] / totals[1])


def solution(mesh):
    return jax.shard_map(
        shards,
        mesh=mesh,
        in_specs=(P("gx", "gy", None), P(None, "gy"), P()),
        out_specs=(P("gx", "gy", None), P("gx", "gy", None), P("gy", "gx")),
        check_vma=False,
    )
```

```python
import functools
import math

import jax
import jax.numpy as jnp
import ml_dtypes
import numpy as np
from jax import lax
from jax.experimental import pallas as pl
from jax.experimental.pallas import tpu as pltpu
from jax.sharding import PartitionSpec as P

LANES = 128
RADIX = 32
GROUPS = RADIX // 2
LENGTH = RADIX * LANES
PAIR = 2 * LANES
BLOCK = 8
BATCH = 4
PARTS = 4
VMEM_BYTES = 56 * 1024 * 1024

CLASSES = [(0, RADIX // 2)] + [(k, RADIX - k) for k in range(1, GROUPS)]


def pair_matrices():
    lane = np.arange(LANES)[None, :]
    place = np.arange(LANES)[:, None]
    matrices = np.zeros((GROUPS, PAIR, PAIR), np.float64)
    for group, classes in enumerate(CLASSES):
        for half, class_index in enumerate(classes):
            angle = 2.0 * math.pi * (lane * (class_index + RADIX * place) % LENGTH) / LENGTH
            both = np.cos(angle) + np.sin(angle)
            turned = np.sin(angle) - np.cos(angle)
            rows = slice(half * LANES, (half + 1) * LANES)
            if group == 0:
                matrices[0, rows, rows] = both
            else:
                matrices[group, rows, :LANES] = both
                matrices[group, rows, LANES:] = turned if half == 0 else -turned
    return matrices


def two_parts(matrices):
    high = matrices.astype(ml_dtypes.bfloat16)
    low = (matrices - high.astype(np.float64)).astype(ml_dtypes.bfloat16)
    return np.stack([high, low])


@functools.cache
def tables():
    ahead = pair_matrices()
    scale = np.full((GROUPS, 1, 1), 1.0 / (2 * LANES * RADIX))
    scale[0] = 1.0 / (LANES * RADIX)
    back = ahead * scale
    return two_parts(ahead), two_parts(np.swapaxes(ahead, 1, 2)), two_parts(back)


def spread(values):
    count = len(values)
    if count == 1:
        return [values[0]], [None]
    if count == 2:
        return [values[0] + values[1], values[0] - values[1]], [None, None]
    quarter, half = count // 4, count // 2
    even_re, even_im = spread(values[0::2])
    odd_re, odd_im = spread(values[1::2])
    out_re, out_im = [None] * (half + 1), [None] * (half + 1)
    out_re[0] = even_re[0] + odd_re[0]
    out_re[half] = even_re[0] - odd_re[0]
    out_re[quarter] = even_re[quarter]
    out_im[quarter] = -odd_re[quarter]
    for k in range(1, quarter):
        cosine, sine = math.cos(2 * math.pi * k / count), math.sin(2 * math.pi * k / count)
        turned_re = cosine * odd_re[k] + sine * odd_im[k]
        turned_im = cosine * odd_im[k] - sine * odd_re[k]
        out_re[k] = even_re[k] + turned_re
        out_im[k] = even_im[k] + turned_im
        out_re[half - k] = even_re[k] - turned_re
        out_im[half - k] = turned_im - even_im[k]
    return out_re, out_im


def gather(real, imag):
    half = len(real) - 1
    if half == 0:
        return [real[0]]
    if half == 1:
        return [real[0] + real[1], real[0] - real[1]]
    count, quarter = 2 * half, half // 2
    even_re, even_im = [None] * (quarter + 1), [None] * (quarter + 1)
    odd_re, odd_im = [None] * (quarter + 1), [None] * (quarter + 1)
    even_re[0] = real[0] + real[half]
    odd_re[0] = real[0] - real[half]
    even_re[quarter] = real[quarter] + real[quarter]
    odd_re[quarter] = -(imag[quarter] + imag[quarter])
    for k in range(1, quarter):
        cosine, sine = math.cos(2 * math.pi * k / count), math.sin(2 * math.pi * k / count)
        even_re[k] = real[k] + real[half - k]
        even_im[k] = imag[k] - imag[half - k]
        diff_re = real[k] - real[half - k]
        diff_im = imag[k] + imag[half - k]
        odd_re[k] = cosine * diff_re - sine * diff_im
        odd_im[k] = sine * diff_re + cosine * diff_im
    values = [None] * count
    values[0::2] = gather(even_re, even_im)
    values[1::2] = gather(odd_re, odd_im)
    return values


def store_groups(ref, at, values):
    real, imag = spread(values)
    for group in range(GROUPS):
        ref[group, at, :LANES] = real[group]
        ref[group, at, LANES:] = imag[group] if group else real[GROUPS]


def load_groups(ref, at):
    pairs = [(ref[group, at, :LANES], ref[group, at, LANES:]) for group in range(GROUPS)]
    real = [pair[0] for pair in pairs] + [pairs[0][1]]
    imag = [None] + [pair[1] for pair in pairs[1:]] + [None]
    return gather(real, imag)


def halves(value):
    high = value.astype(jnp.bfloat16)
    return high, (value - high.astype(jnp.float32)).astype(jnp.bfloat16)


def dot(left, right, right_axis=0):
    return lax.dot_general(
        left, right, (((1,), (right_axis,)), ((), ())), preferred_element_type=jnp.float32
    )


def times_table(value, table_ref, group):
    high, low = halves(value)
    return dot(high, table_ref[0, group]) + (
        dot(low, table_ref[0, group]) + dot(high, table_ref[1, group])
    )


def strip_at(index):
    return pl.ds(pl.multiple_of(index * BLOCK, BLOCK), BLOCK)


def lanes_of(index):
    return slice(index * LANES, (index + 1) * LANES)


def step_order(count):
    half = count // 2
    pairs = [(near, half + near) for near in range(half)]
    return [0] + [step for pair in pairs[1:] for step in pair] + [half]


def taken(refs, kinds, count):
    chunks = []
    for stacked in kinds:
        held = 1 if stacked else count
        chunks.append(list(refs[:held]))
        refs = refs[held:]
    return chunks, refs


def view(chunk, stacked, me, step):
    if stacked:
        return step, chunk[0].at[step]
    return me ^ step_order(len(chunk))[step], chunk[step]


def forward_x(count, cuts, kinds, me_ref, noise_ref, table_ref, *refs):
    outs, (group_ref, spectrum_ref) = taken(refs, kinds, count)
    rows = noise_ref.shape[1]
    share = LANES // count
    me = me_ref[0]

    def strip(index, carry):
        at = strip_at(index)
        store_groups(group_ref, at, [noise_ref[0, at, lanes_of(a)] for a in range(RADIX)])
        return carry

    lax.fori_loop(0, rows // BLOCK, strip, 0, unroll=2)
    for cut, (first, last) in enumerate(cuts):

        def group_step(group, carry, cut=cut, first=first):
            high, low = halves(group_ref[group])
            both = dot(table_ref[0, group], jnp.concatenate([high, low], axis=0), 1)
            spectrum_ref[...] = (both[:, :rows] + both[:, rows:]) + dot(table_ref[1, group], high, 1)
            for step in range(count):
                place, out = view(outs[cut], kinds[cut], me, step)
                for half in range(2):
                    source = pl.multiple_of(half * LANES + place * share, share)
                    target = pl.multiple_of(((group - first) * 2 + half) * share, share)
                    out[pl.ds(target, share), :] = spectrum_ref[pl.ds(source, share), :]
            return carry

        lax.fori_loop(first, last, group_step, 0, unroll=4)


def filter_y(count, in_cuts, in_kinds, out_cuts, out_kinds, gains, me_ref, *refs):
    ins, refs = taken(refs, in_kinds, count)
    gain_refs, (ahead_ref, back_ref) = refs[:gains], refs[gains : gains + 2]
    outs, (field_ref, group_ref) = taken(refs[gains + 2 :], out_kinds, count)
    rows = field_ref.shape[1]
    per = field_ref.shape[2] // LANES
    me = me_ref[0]
    for chunk, stacked, (first, last) in zip(ins, in_kinds, in_cuts):
        for step in range(count):
            place, piece = view(chunk, stacked, me, step)
            field_ref[place, :, first:last] = piece[...]

    def ahead_strip(index, carry):
        at = strip_at(index)
        values = [field_ref[a // per, at, lanes_of(a % per)] for a in range(RADIX)]
        store_groups(group_ref, at, values)
        return carry

    lax.fori_loop(0, rows // BLOCK, ahead_strip, 0, unroll=2)

    def group_step(group, carry):
        spectrum = times_table(group_ref[group], ahead_ref, group)
        other = jnp.where(group == 0, RADIX // 2, RADIX - group)
        columns = [
            pl.ds(pl.multiple_of(place * LANES, LANES), LANES) for place in (group, other)
        ]
        gain = jnp.concatenate(
            [
                jnp.concatenate([ref[0, :, column] for ref in gain_refs], axis=0)
                for column in columns
            ],
            axis=1,
        )
        group_ref[group] = times_table(spectrum * gain, back_ref, group)
        return carry

    lax.fori_loop(0, GROUPS, group_step, 0, unroll=4)

    def back_strip(index, carry):
        at = strip_at(index)
        for a, value in enumerate(load_groups(group_ref, at)):
            field_ref[a // per, at, lanes_of(a % per)] = value
        return carry

    lax.fori_loop(0, rows // BLOCK, back_strip, 0, unroll=2)
    for chunk, stacked, (first, last) in zip(outs, out_kinds, out_cuts):
        for step in range(count):
            place, piece = view(chunk, stacked, me, step)
            piece[...] = field_ref[place, :, first:last]


def inverse_x(
    count, cuts, kinds, lanes, layer, start, has_before, has_after, aliased, me_ref, offsets_ref, *refs
):
    ins, refs = taken(refs, kinds, count)
    table_hbm, refs = refs[0], refs[1:]
    edges = has_before + has_after
    edge_hbm, refs = refs[:edges], refs[edges:]
    if aliased:
        refs = refs[2:]
    face_x_hbm, face_y_hbm, sums_ref, first_ref, last_ref, *scratch = refs
    piece_ref, table_ref, edge_ref, group_ref, upper_ref, lower_ref = scratch[:6]
    face_x, face_y, column_ref, in_sems, edge_sems, out_sems = scratch[6:]
    rows = face_x.shape[0]
    tiles = rows // BLOCK
    share = LANES // count
    me = me_ref[0]
    lead = 1 if has_before else 0
    made = tiles - 1 + lead + (1 if has_after else 0)
    width = RADIX * LANES

    def arrivals(batch):
        group = BATCH * batch
        copies = [
            pltpu.make_async_copy(
                table_hbm.at[part, pl.ds(group, BATCH)],
                table_ref.at[part, pl.ds(group, BATCH)],
                in_sems.at[batch, part],
            )
            for part in range(2)
        ]
        cut = max(number for number in range(len(cuts)) if cuts[number][0] <= group)
        depth = 2 * share * BATCH
        for step in range(count):
            place, piece = view(ins[cut], kinds[cut], me, step)
            copies.append(
                pltpu.make_async_copy(
                    piece.at[
                        pl.ds(2 * share * (group - cuts[cut][0]), depth), pl.ds(lanes[cut], rows)
                    ],
                    piece_ref.at[place, pl.ds(2 * share * group, depth), :],
                    in_sems.at[batch, 2 + step],
                )
            )
        return copies

    batches = [arrivals(batch) for batch in range(GROUPS // BATCH)]
    edge_copies = [
        pltpu.make_async_copy(edge_hbm[edge], edge_ref.at[edge], edge_sems.at[edge])
        for edge in range(edges)
    ]
    for copies in batches + [edge_copies]:
        for copy in copies:
            copy.start()

    def group_step(group, carry):
        parts = []
        for half in range(2):
            at = pl.ds(pl.multiple_of((2 * group + half) * share, share), share)
            parts.append(piece_ref[:, at, :].reshape(LANES, rows))
        stacked = jnp.concatenate(parts, axis=0)
        group_ref[group] = times_table(stacked.T, table_ref, group)
        return carry

    for batch, copies in enumerate(batches):
        for copy in copies:
            copy.wait()
        lax.fori_loop(BATCH * batch, BATCH * (batch + 1), group_step, 0, unroll=BATCH)

    def raised(field, at, a):
        upper_ref[at, lanes_of(a)] = jnp.exp(field)
        lower_ref[at, lanes_of(a)] = jnp.exp(-field)

    def field_strip(index, carry, copy_ref=None):
        at = strip_at(index)
        to = strip_at(index + lead)
        for a, value in enumerate(load_groups(group_ref, at)):
            raised(value, to, a)
            if copy_ref is not None:
                copy_ref[:, lanes_of(a)] = value
        return carry

    field_strip(0, 0, first_ref)
    lax.fori_loop(1, tiles - 1, field_strip, 0, unroll=2)
    field_strip(tiles - 1, 0, last_ref)
    for copy in edge_copies:
        copy.wait()
    for a in range(RADIX):
        if has_before:
            raised(edge_ref[0, :, lanes_of(a)], slice(0, BLOCK), a)
        if has_after:
            end = (lead + tiles) * BLOCK
            raised(edge_ref[edges - 1, :, lanes_of(a)], slice(end, end + BLOCK), a)

    row_index = lax.broadcasted_iota(jnp.int32, (BLOCK, LANES), 0)
    lane_index = lax.broadcasted_iota(jnp.int32, (BLOCK, LANES), 1)
    own_rows = row_index >= offsets_ref[0]
    last_row = row_index == BLOCK - 1
    last_lane = lane_index == LANES - 1

    def x_strip(index, carry):
        at = strip_at(index)
        here = [lower_ref[strip_at(index + lead), lanes_of(a)] for a in range(RADIX)]
        moved = [pltpu.roll(value, LANES - 1, 1) for value in here]
        for a in range(RADIX):
            beside = jnp.where(last_lane, moved[(a + 1) % RADIX], moved[a])
            face_x[at, lanes_of(a)] = 2.0 / (here[a] + beside)
        return carry

    def add_row(kind, index, a, value):
        at = strip_at(index // BLOCK)
        total = jnp.sum(value, axis=0, keepdims=True)
        column_ref[kind, at, lanes_of(a)] = jnp.where(
            row_index == index % BLOCK, total, column_ref[kind, at, lanes_of(a)]
        )

    def y_strip(index, carry):
        at = strip_at(index)
        then = strip_at(index + 1)
        for a in range(RADIX):
            here, below = lower_ref[at, lanes_of(a)], lower_ref[then, lanes_of(a)]
            moved = pltpu.roll(jnp.where(row_index == 0, below, here), BLOCK - 1, 0)
            face_y[at, lanes_of(a)] = 2.0 / (here + moved)
            add_row(1, index, a, jnp.where(own_rows, here, below))
            here, below = upper_ref[at, lanes_of(a)], upper_ref[then, lanes_of(a)]
            add_row(0, index, a, jnp.where(own_rows, here, below))
        return carry

    leaving = []
    faces = [(x_strip, tiles, start, face_x, face_x_hbm)]
    faces.append((y_strip, made, start - BLOCK * lead, face_y, face_y_hbm))
    for part in range(PARTS):
        for number, (strip, total, origin, face, face_hbm) in enumerate(faces):
            begin = part * (tiles // PARTS)
            end = total if part == PARTS - 1 else begin + tiles // PARTS
            lax.fori_loop(begin, end, strip, 0, unroll=2)
            size = BLOCK * (end - begin)
            copy = pltpu.make_async_copy(
                face.at[pl.ds(BLOCK * begin, size), :],
                face_hbm.at[layer, pl.ds(origin + BLOCK * begin, size), :],
                out_sems.at[number, part],
            )
            copy.start()
            leaving.append(copy)

    column_ref[:, :, width:] = column_ref[:, :, :LANES]
    reach = BLOCK * LANES + LANES
    lane = lax.broadcasted_iota(jnp.int32, (reach, LANES), 0)
    block = lax.broadcasted_iota(jnp.int32, (reach, LANES), 1)
    inside = lane - offsets_ref[1] - BLOCK * block
    chosen = jnp.where((inside >= 0) & (inside < BLOCK), 1.0, 0.0).astype(jnp.bfloat16)
    for kind in range(2):
        for part in range(width // (BLOCK * LANES)):
            at = BLOCK * LANES * part
            high, low = halves(column_ref[kind, :, at : at + reach])
            sums_ref[kind, :, lanes_of(part)] = dot(high, chosen) + dot(low, chosen)
    for copy in leaving:
        copy.wait()


def exchange(chunk, axis):
    if not isinstance(chunk, list):
        return lax.all_to_all(chunk, axis, 0, 0, tiled=True)
    count = len(chunk)
    arrived = [chunk[0]]
    for piece, step in zip(chunk[1:], step_order(count)[1:]):
        pairs = [(device, device ^ step) for device in range(count)]
        arrived.append(lax.ppermute(piece, axis, pairs))
    return arrived


def flat(chunks):
    return [ref for chunk in chunks for ref in (chunk if isinstance(chunk, list) else [chunk])]


def chunked(refs, kinds, count):
    chunks, _ = taken(refs, kinds, count)
    return [chunk[0] if stacked else chunk for chunk, stacked in zip(chunks, kinds)]


def kinds_of(chunks):
    return [not isinstance(chunk, list) for chunk in chunks]


def block_specs(kinds, count, shapes, place_of):
    specs = []
    for number, (stacked, shape) in enumerate(zip(kinds, shapes)):
        place = place_of(number)
        if stacked:
            specs.append(pl.BlockSpec((count, *shape), lambda i, place=place: (0, *place(i))))
        else:
            specs += [pl.BlockSpec(shape, place)] * count
    return specs


def whole_shapes(kinds, count, shapes):
    made = []
    for stacked, shape in zip(kinds, shapes):
        if stacked:
            made.append(jax.ShapeDtypeStruct((count, *shape), jnp.float32))
        else:
            made += [jax.ShapeDtypeStruct(shape, jnp.float32)] * count
    return made


def scalars():
    return pl.BlockSpec(memory_space=pltpu.SMEM)


def params():
    return pltpu.CompilerParams(vmem_limit_bytes=VMEM_BYTES)


def cost(rows, micros):
    return pl.CostEstimate(
        flops=int(rows * micros * 1.15e9 / 256),
        bytes_accessed=rows * LENGTH * 8,
        transcendentals=0,
    )


def run_forward(me, noise, layer, span, cuts, kinds, count, table):
    share = LANES // count
    first, last = span
    step_rows = LANES
    depths = [2 * share * (end - begin) for begin, end in cuts]
    offset = first // step_rows
    outs = pl.pallas_call(
        functools.partial(forward_x, count, cuts, kinds),
        grid=((last - first) // step_rows,),
        in_specs=[
            scalars(),
            pl.BlockSpec((1, step_rows, LENGTH), lambda i: (layer, i + offset, 0)),
            pl.BlockSpec(table.shape, lambda i: (0, 0, 0, 0), pipeline_mode=pl.Buffered(1)),
        ],
        out_specs=block_specs(
            kinds, count, [(depth, step_rows) for depth in depths], lambda n: lambda i: (0, i)
        ),
        out_shape=whole_shapes(kinds, count, [(depth, last - first) for depth in depths]),
        scratch_shapes=[
            pltpu.VMEM((GROUPS, step_rows, PAIR), jnp.float32),
            pltpu.VMEM((PAIR, step_rows), jnp.float32),
        ],
        compiler_params=params(),
        cost_estimate=cost(last - first, 9),
        name="forward_x",
    )(me, noise, table)
    return chunked(outs, kinds, count)


def run_filter(me, chunks, in_cuts, out_cuts, out_kinds, count, gain, span, ahead, back):
    first_row, rows = span.start, span.stop - span.start
    step_rows = min(rows, LANES)
    lane_count = LENGTH // count
    share = LANES // count
    offset = first_row // step_rows
    in_kinds = kinds_of(chunks)
    skips = [offset if flat([chunk])[0].shape[-2] > rows else 0 for chunk in chunks]
    table_spec = pl.BlockSpec(ahead.shape, lambda i: (0, 0, 0, 0), pipeline_mode=pl.Buffered(1))
    gains = step_rows // share

    def gain_place(number):
        def place(i):
            group = (i + offset) * (gains // 2) + number // 2
            if number % 2 == 0:
                return (group, 0, 0)
            return (jnp.where(group == 0, RADIX // 2, RADIX - group), 0, 0)

        return place

    outs = pl.pallas_call(
        functools.partial(filter_y, count, in_cuts, in_kinds, out_cuts, out_kinds, gains),
        grid=(rows // step_rows,),
        in_specs=[scalars()]
        + block_specs(
            in_kinds,
            count,
            [(step_rows, cut[1] - cut[0]) for cut in in_cuts],
            lambda n: lambda i: (i + skips[n], 0),
        )
        + [pl.BlockSpec((1, share, LENGTH), gain_place(n)) for n in range(gains)]
        + [table_spec, table_spec],
        out_specs=block_specs(
            out_kinds,
            count,
            [(step_rows, cut[1] - cut[0]) for cut in out_cuts],
            lambda n: lambda i: (i, 0),
        ),
        out_shape=whole_shapes(out_kinds, count, [(rows, cut[1] - cut[0]) for cut in out_cuts]),
        scratch_shapes=[
            pltpu.VMEM((count, step_rows, lane_count), jnp.float32),
            pltpu.VMEM((GROUPS, step_rows, PAIR), jnp.float32),
        ],
        compiler_params=params(),
        cost_estimate=cost(rows, 16),
        name="filter_y",
    )(me, *flat(chunks), *[gain] * gains, ahead, back)
    return chunked(outs, out_kinds, count)


def run_inverse(
    me, offsets, chunks, lane_starts, cuts, count, layer, span, table, before, after, faces, shape
):
    first, last = span
    rows = last - first
    tiles = rows // BLOCK
    made = tiles - 1 + (before is not None) + (after is not None)
    padded = -(-made // 16) * 16
    held = tiles + (before is not None) + (after is not None)
    kinds = kinds_of(chunks)
    extra = [value for value in (before, after) if value is not None]
    outside = pl.BlockSpec(memory_space=pl.ANY)
    inside = pl.BlockSpec(memory_space=pltpu.VMEM)
    in_specs = [scalars(), scalars()] + [outside] * (len(flat(chunks)) + 1 + len(extra))
    aliases = {}
    if faces is not None:
        aliases = {len(in_specs): 0, len(in_specs) + 1: 1}
        in_specs += [outside] * 2
    face = jax.ShapeDtypeStruct(shape, jnp.float32)
    tile = jax.ShapeDtypeStruct((BLOCK, LENGTH), jnp.float32)
    sums_shape = (2, padded, LENGTH // BLOCK)
    face_x, face_y, sums, first_tile, last_tile = pl.pallas_call(
        functools.partial(
            inverse_x,
            count,
            cuts,
            kinds,
            lane_starts,
            layer,
            first,
            before is not None,
            after is not None,
            faces is not None,
        ),
        in_specs=in_specs,
        out_specs=[outside, outside, inside, inside, inside],
        out_shape=[face, face, jax.ShapeDtypeStruct(sums_shape, jnp.float32), tile, tile],
        scratch_shapes=[
            pltpu.VMEM((count, LENGTH // count, rows), jnp.float32),
            pltpu.VMEM(table.shape, table.dtype),
            pltpu.VMEM((max(len(extra), 1), BLOCK, LENGTH), jnp.float32),
            pltpu.VMEM((GROUPS, rows, PAIR), jnp.float32),
            pltpu.VMEM((held * BLOCK, LENGTH), jnp.float32),
            pltpu.VMEM((held * BLOCK, LENGTH), jnp.float32),
            pltpu.VMEM((rows, LENGTH), jnp.float32),
            pltpu.VMEM((made * BLOCK, LENGTH), jnp.float32),
            pltpu.VMEM((2, padded, LENGTH + LANES), jnp.float32),
            pltpu.SemaphoreType.DMA((GROUPS // BATCH, 2 + count)),
            pltpu.SemaphoreType.DMA((2,)),
            pltpu.SemaphoreType.DMA((2, PARTS)),
        ],
        input_output_aliases=aliases,
        compiler_params=params(),
        cost_estimate=cost(rows, 18),
        name="inverse_x",
    )(me, offsets, *flat(chunks), table, *extra, *(faces or ()))
    return (face_x, face_y), sums[:, :made], first_tile, last_tile


def arranged(amplitude, count):
    share = LANES // count
    table = amplitude.reshape(LANES, RADIX, RADIX * share).transpose(1, 0, 2)
    table = lax.optimization_barrier(table).reshape(LENGTH, RADIX * share).T
    return lax.optimization_barrier(table).reshape(share, RADIX, LENGTH).transpose(1, 0, 2)


def sum_scattered(values, axis):
    count = lax.axis_size(axis)
    me = lax.axis_index(axis)
    width = values.shape[-1] // count
    total = lax.dynamic_slice_in_dim(values, me * width, width, values.ndim - 1)
    for step in range(1, count):
        part = lax.dynamic_slice_in_dim(values, (me ^ step) * width, width, values.ndim - 1)
        total = total + lax.ppermute(part, axis, [(d, d ^ step) for d in range(count)])
    return total


def shards(white_noise, amplitude, offsets):
    layers, rows, _ = white_noise.shape
    count = lax.axis_size("gy")
    share = LANES // count
    me = lax.axis_index("gy").reshape(1)
    analysis, ahead, back = [jnp.asarray(table) for table in tables()]
    arrive_spans = [(0, LANES), (LANES, rows)]
    half = rows // 2
    leave_spans = [(0, half), (half, rows)]
    done_spans = leave_spans
    cuts = [(0, GROUPS // 2), (GROUPS // 2, GROUPS)]
    every = [(0, GROUPS)]
    gain = None
    faces = None
    totals = None
    for layer in range(layers):
        (early,) = run_forward(me, white_noise, layer, arrive_spans[0], every, [False], count, analysis)
        early = exchange(early, "gy")
        sent = run_forward(me, white_noise, layer, arrive_spans[1], cuts, [False, False], count, analysis)
        if gain is None:
            amplitude, sent = lax.optimization_barrier((amplitude, sent))
            gain = arranged(amplitude, count)
        late = [exchange(part, "gy") for part in sent]
        returned = []
        for cut, (first, last) in enumerate(cuts):
            span = slice(2 * share * first, 2 * share * last)
            out_cuts, out_kinds = ([(0, rows)], [False]) if cut == 0 else (leave_spans, [False, False])
            made = run_filter(
                me,
                [early, late[cut]],
                arrive_spans,
                out_cuts,
                out_kinds,
                count,
                gain,
                span,
                ahead,
                back,
            )
            returned.append([exchange(part, "gy") for part in made])
        before = after = None
        sums = []
        for index, span in enumerate(done_spans):
            final = index == len(done_spans) - 1
            chunks = [returned[0][0], returned[1][1 if final else 0]]
            lane_starts = [span[0], 0 if final else span[0]]
            if final:
                pairs = [(device, (device - 1) % count) for device in range(count)]
                after = lax.ppermute(first_tile, "gy", pairs)
            faces, part, head, before_next = run_inverse(
                me,
                offsets,
                chunks,
                lane_starts,
                cuts,
                count,
                layer,
                span,
                back,
                before,
                after,
                faces,
                white_noise.shape,
            )
            sums.append(part)
            before = before_next
            if index == 0:
                first_tile = head
        blocks = jnp.concatenate(sums, axis=1)
        totals = blocks if totals is None else totals + blocks
    totals = sum_scattered(totals, "gx")
    return faces[0], faces[1], jnp.sqrt(totals[0] / totals[1])


def solution(mesh):
    return jax.shard_map(
        shards,
        mesh=mesh,
        in_specs=(P("gx", "gy", None), P(None, "gy"), P()),
        out_specs=(P("gx", "gy", None), P("gx", "gy", None), P("gy", "gx")),
        check_vma=False,
    )
```
